32 devices in a mesh: groups: 2 (over y), ctx: 4 (over z), tp: 4 (over x, core).
Axes of the slice: x: 2, y: 2, z: 4, core: 2. Of those that a mesh axis runs over, the one named last changes fastest.
Arguments:
- x_in: bfloat16 [4096, 4096], P(('groups', 'ctx'), 'tp'), parts along dimension 0, may hold values from -6 to 6
- z_in: bfloat16 [4096, 4096], P(('groups', 'ctx'), 'tp'), parts along dimension 0, may hold values from -6 to 6
- b_in: bfloat16 [4096, 512], P(('groups', 'ctx'), 'tp'), parts along dimension 0, may hold values from -6 to 6
- c_in: bfloat16 [4096, 512], P(('groups', 'ctx'), 'tp'), parts along dimension 0, may hold values from -6 to 6
- dt_in: bfloat16 [4096, 64], P(('groups', 'ctx'), 'tp'), parts along dimension 0, may hold values from -4 to 14
- conv_x: bfloat16 [4, 4096], P(None, 'tp'), may hold values from -3 to 3
- conv_bc: bfloat16 [2, 4, 512], P(None, None, 'tp'), may hold values from -3 to 3
- dt_bias: float32 [64], P('tp'), may hold values from -13 to -2
- a_log: float32 [64], P('tp'), may hold values from -0.7 to 0.4
- d_skip: float32 [64], P('tp'), may hold values from 0.5 to 1.5
- norm_gain: bfloat16 [4096], P('tp'), may hold values from 0.5 to 1.5
- out_weight: bfloat16 [4096, 4096], P('ctx', 'tp'), may hold values from -0.09375 to 0.09375
Outputs:
- mixed: bfloat16 [4096, 4096], P(('groups', 'ctx'), 'tp'), parts along dimension 0
The draws below stay inside these ranges and needn't reach their ends.
There are 2 independent parts, one for each index of `groups`. The reference program is written for one: setup_inputs(seed, part) draws one part's arguments, and reference() takes and returns one part's arrays. A program takes and returns all parts, laid end to end along the dimension named above; an argument that names none is the same for every part. Nothing has to cross between parts.
All inputs are finite; a program needn't handle non-finite values.
Results may differ from the reference program's by a relative error of at most 0.0059.
Values may be sent and summed in bfloat16 or wider, within the bound.
A program may use at most 128 MiB of HBM per device.

```python
import math
import jax
import jax.numpy as jnp
from jax import lax

HEADS = 64
HEAD_DIM = 64
STATE = 128
GROUPS = 4
OUT_WIDTH = 4096
SPAN = 256
CONV_WIDTH = 4
INNER = 4096
TOKENS = 2048


def draw_dt_bias(key, part):
    key_class, key_slow, key_fast = jax.random.split(key, 3)
    picked = jax.random.uniform(key_class, (HEADS,))
    share = 0.5
    slow_value = -math.log(float(TOKENS)) + jax.random.uniform(key_slow, (HEADS,), minval=-0.3, maxval=0.3)
    fast_value = jax.random.uniform(key_fast, (HEADS,), minval=-4.0, maxval=-3.0)
    return jnp.where(picked < share, slow_value, fast_value).astype(jnp.float32)


def draw_dt_in(key, part):
    key_noise, key_offset, key_spots = jax.random.split(key, 3)
    noise = 0.5 * jax.random.normal(key_noise, (TOKENS, HEADS))
    offsets = jax.random.uniform(key_offset, (TOKENS // SPAN, 1, HEADS), minval=-0.7, maxval=0.7)
    offsets = jnp.broadcast_to(offsets, (TOKENS // SPAN, SPAN, HEADS)).reshape(TOKENS, HEADS)
    spots = jax.random.randint(key_spots, (6,), 0, TOKENS)
    struck = jnp.any(jnp.arange(TOKENS)[:, None] == spots[None, :], axis=1)
    jump_size = math.log(0.4 * TOKENS)
    raw_value = noise + offsets + jnp.where(struck[:, None], jump_size, 0.0)
    return jnp.clip(raw_value, -4.0, 14.0).astype(jnp.float32).astype(jnp.bfloat16)


def block_levels(stream_key, extent, cuts, least, largest):
    level, own = 1.0, jax.random.fold_in(stream_key, 6)
    for axis_at, shards_of in cuts:
        steps = jnp.exp(jax.random.uniform(jax.random.fold_in(own, axis_at), (shards_of,), jnp.float32, least / len(cuts), largest / len(cuts)))
        level = level * jnp.repeat(steps, extent[axis_at] // shards_of).reshape([-1 if axis == axis_at else 1 for axis in range(len(extent))])
    return level


def bell_draw(rng, shape, deviation, most, pieces=(), kind=jnp.bfloat16):
    loudness = block_levels(rng, shape, pieces, -0.22, 0.18) if pieces else 1.0
    entries = jax.random.normal(rng, shape, jnp.float32) * deviation * loudness
    return jnp.minimum(jnp.maximum(entries, -most), most).astype(kind)


def setup_inputs(seed: int = 0, part: int = 0) -> dict:
    seeds = jax.random.split(jax.random.key(seed), 13)
    own_keys = jax.random.split(jax.random.fold_in(seeds[12], part), 13)
    return {
        "x_in": bell_draw(own_keys[0], (TOKENS, INNER), 1.0, 6.0, ((0, 4), (1, 4))),
        "z_in": bell_draw(own_keys[1], (TOKENS, INNER), 1.0, 6.0, ((0, 4), (1, 4))),
        "b_in": bell_draw(own_keys[2], (TOKENS, GROUPS * STATE), 1.0, 6.0, ((0, 4), (1, 4))),
        "c_in": bell_draw(own_keys[3], (TOKENS, GROUPS * STATE), 1.0, 6.0, ((0, 4), (1, 4))),
        "dt_in": draw_dt_in(jax.random.fold_in(jax.random.fold_in(seeds[12], part), 71), part),
        "conv_x": bell_draw(seeds[5], (CONV_WIDTH, INNER), CONV_WIDTH ** -0.5, 3.0, ((1, 4),)),
        "conv_bc": bell_draw(seeds[6], (2, CONV_WIDTH, GROUPS * STATE), CONV_WIDTH ** -0.5, 3.0, ((2, 4),)),
        "dt_bias": draw_dt_bias(jax.random.fold_in(seeds[12], 71), part),
        "a_log": jnp.clip(-0.7 + 1.1 * jax.random.uniform(seeds[8], (HEADS,), jnp.float32) ** block_levels(seeds[8], (HEADS,), ((0, 4),), -0.2, 0.2), -0.7, 0.4),
        "d_skip": jnp.clip(0.5 + 1.0 * jax.random.uniform(seeds[9], (HEADS,), jnp.float32) ** block_levels(seeds[9], (HEADS,), ((0, 4),), -0.2, 0.2), 0.5, 1.5),
        "norm_gain": jnp.clip(1.0 + 0.1 * jax.random.normal(seeds[10], (INNER,), jnp.float32), 0.5, 1.5).astype(jnp.bfloat16),
        "out_weight": bell_draw(seeds[11], (INNER, OUT_WIDTH), INNER ** -0.5, 0.09375, ((0, 4), (1, 4))),
    }


EPS = 1e-05

def causal_conv(extended, taps, length):
    summed = jnp.zeros((length, extended.shape[1]), jnp.float32)
    for kernel_tap in range(taps.shape[0]):
        summed = summed + extended[kernel_tap:kernel_tap + length].astype(jnp.float32) * taps[kernel_tap].astype(jnp.float32)
    return jax.nn.silu(summed).astype(jnp.bfloat16)

def span_parts(x_rows, b_rows, c_rows, step_span, decay_rate, groups, widen):
    length = x_rows.shape[0]
    head_count = step_span.shape[1]
    per_group = head_count // groups
    state_size = b_rows.shape[1] // groups
    b_groups = b_rows.reshape(length, groups, state_size)
    c_groups = c_rows.reshape(length, groups, state_size)
    x_heads = x_rows.reshape(length, head_count, -1)
    cumulative = jnp.cumsum(step_span * decay_rate[None, :], axis=0)
    if widen:
        scores = jnp.einsum('tgn,sgn->gts', c_groups.astype(jnp.float32), b_groups.astype(jnp.float32))
    else:
        scores = jnp.einsum('tgn,sgn->gts', c_groups, b_groups, preferred_element_type=jnp.float32)
    positions = jnp.arange(length)
    causal = positions[:, None] >= positions[None, :]
    transposed = cumulative.T
    gaps = jnp.where(causal[None], transposed[:, :, None] - transposed[:, None, :], -1e+30)
    mixing = (jnp.repeat(scores, per_group, axis=0) * jnp.exp(gaps) * step_span.T[:, None, :]).astype(jnp.bfloat16)
    if widen:
        diagonal_part = jnp.einsum('hts,shp->thp', mixing.astype(jnp.float32), x_heads.astype(jnp.float32))
    else:
        diagonal_part = jnp.einsum('hts,shp->thp', mixing, x_heads, preferred_element_type=jnp.float32)
    to_end = jnp.exp(cumulative[-1][None, :] - cumulative) * step_span
    weighted = (x_heads.astype(jnp.float32) * to_end[:, :, None]).astype(jnp.bfloat16)
    b_heads = jnp.repeat(b_groups, per_group, axis=1)
    if widen:
        local_state = jnp.einsum('shp,shn->hpn', weighted.astype(jnp.float32), b_heads.astype(jnp.float32))
    else:
        local_state = jnp.einsum('shp,shn->hpn', weighted, b_heads, preferred_element_type=jnp.float32)
    return (diagonal_part.reshape(length, -1), local_state, cumulative)

def carried(c_rows, cumulative, entering, groups):
    length = c_rows.shape[0]
    head_count = cumulative.shape[1]
    state_size = entering.shape[2]
    c_heads = jnp.repeat(c_rows.reshape(length, groups, state_size), head_count // groups, axis=1).astype(jnp.float32)
    summed = jnp.einsum('thn,hpn->thp', c_heads, entering, precision=lax.Precision.HIGHEST)
    return (summed * jnp.exp(cumulative)[:, :, None]).reshape(length, -1)

def finish(ssd_part, x_rows, gate_rows, d_skip, norm_gain, groups):
    length, inner_here = x_rows.shape
    head_count = d_skip.shape[0]
    skip_term = (x_rows.astype(jnp.float32).reshape(length, head_count, -1) * d_skip[None, :, None]).reshape(length, inner_here)
    gated = (ssd_part + skip_term) * jax.nn.silu(gate_rows.astype(jnp.float32))
    grouped = gated.reshape(length, groups, -1)
    scale = lax.rsqrt(lax.optimization_barrier(jnp.mean(grouped * grouped, axis=2, keepdims=True)) + EPS)
    return ((grouped * scale).reshape(length, inner_here) * norm_gain.astype(jnp.float32)).astype(jnp.bfloat16)

def reference(x_in, z_in, b_in, c_in, dt_in, conv_x, conv_bc, dt_bias, a_log, d_skip, norm_gain, out_weight):
    rim_rows = CONV_WIDTH - 1
    xs = causal_conv(jnp.concatenate([jnp.zeros((rim_rows, x_in.shape[1]), jnp.bfloat16), x_in], 0), conv_x, TOKENS)
    bs = causal_conv(jnp.concatenate([jnp.zeros((rim_rows, b_in.shape[1]), jnp.bfloat16), b_in], 0), conv_bc[0], TOKENS)
    cs = causal_conv(jnp.concatenate([jnp.zeros((rim_rows, c_in.shape[1]), jnp.bfloat16), c_in], 0), conv_bc[1], TOKENS)
    step_size = jax.nn.softplus(dt_in.astype(jnp.float32) + dt_bias[None, :])
    decay_rate = -jnp.exp(a_log)

    def advance(entering, span_index):
        first_row = (span_index * SPAN).astype(jnp.int32)

        def take_rows(array):
            return lax.dynamic_slice_in_dim(array, first_row, SPAN, 0)
        c_rows = take_rows(cs)
        x_rows = take_rows(xs)
        diagonal_part, local_state, cumulative = span_parts(x_rows, take_rows(bs), c_rows, take_rows(step_size), decay_rate, GROUPS, True)
        ssd_part = diagonal_part + carried(c_rows, cumulative, entering, GROUPS)
        following = jnp.exp(cumulative[-1])[:, None, None] * entering + local_state
        return (following, finish(ssd_part, x_rows, take_rows(z_in), d_skip, norm_gain, GROUPS))
    start_state = jnp.zeros((HEADS, HEAD_DIM, STATE), jnp.float32)
    unused, normed = lax.scan(advance, start_state, jnp.arange(TOKENS // SPAN, dtype=jnp.int32))
    normed = normed.reshape(TOKENS, INNER)
    return jnp.dot(normed, out_weight, preferred_element_type=jnp.float32).astype(jnp.bfloat16)
```

```python
import functools
import jax
import jax.numpy as jnp
from jax import lax
from jax.experimental import pallas as pl
from jax.experimental.pallas import tpu as pltpu
from jax.sharding import PartitionSpec as P

STATE = 128
SPAN = 256
EPS = 1e-05
RIM = 16
TILE = 256
MESH = pl.DeviceIdType.MESH
F32 = jnp.float32
BF16 = jnp.bfloat16


def dot(a, b):
    return jnp.dot(a, b, preferred_element_type=F32)


def silu(v):
    return v / (1.0 + jnp.exp(-v))


def spread(value, table):
    high = value.astype(BF16)
    low = (value - high.astype(F32)).astype(BF16)
    return dot(high, table) + dot(low, table)


def kernel(
    n, chunks,
    x_ref, z_ref, b_ref, c_ref, dt_ref, conv_ref, convbc_ref, bias_ref, alog_ref, skip_ref, gain_ref, w_ref,
    o_ref,
    wfull, nall, xe, xs, bs, cs, ssd, state0, state1, entering, outgoing, halo_x, halo_b, halo_c,
    own_sem, halo_send, halo_recv, chain_send, chain_recv,
    right_send, right_recv, left_send, left_recv,
    yr_send, yr_recv, yl_send, yl_recv,
    tp_send, tp_recv,
):
    g = lax.axis_index("groups")
    me = lax.axis_index("ctx")
    p = lax.axis_index("tp")
    other = 1 - g
    near = p + 1 - 2 * lax.rem(p, 2)
    far = lax.rem(p + 2, 4)
    rows, inner = x_ref.shape
    heads = dt_ref.shape[1]
    width = inner // heads
    spans = rows // SPAN
    depth = w_ref.shape[0]
    half = depth // 2
    piece = half // chunks
    has_left, has_right = me > 0, me < n - 1

    barrier = pltpu.get_barrier_semaphore()
    for device in ({"groups": other}, {"tp": near}, {"tp": far}):
        pl.semaphore_signal(barrier, inc=1, device_id=device, device_id_type=MESH)

    @pl.when(has_left)
    def _():
        pl.semaphore_signal(barrier, inc=1, device_id={"ctx": me - 1}, device_id_type=MESH)

    @pl.when(has_right)
    def _():
        pl.semaphore_signal(barrier, inc=1, device_id={"ctx": me + 1}, device_id_type=MESH)

    pl.semaphore_wait(barrier, 3 + has_left.astype(jnp.int32) + has_right.astype(jnp.int32))

    def remote(src, dst, send, recv, device):
        return pltpu.make_async_remote_copy(
            src_ref=src, dst_ref=dst, send_sem=send, recv_sem=recv, device_id=device, device_id_type=MESH
        )

    def halo(i):
        src = (x_ref, b_ref, c_ref)[i].at[pl.ds(rows - RIM, RIM)]
        dst = (halo_x, halo_b, halo_c)[i]
        return remote(src, dst, halo_send.at[i], halo_recv.at[i], {"ctx": me + 1})

    @pl.when(has_right)
    def _():
        for i in range(3):
            halo(i).start()

    def strip(block, part, k):
        return pl.ds(pl.multiple_of(block * depth + part * half + k * piece, 16), piece)

    def own_strip(k):
        return pl.ds(pl.multiple_of(g * half + k * piece, 16), piece)

    def go_right(s, k):
        src = w_ref.at[own_strip(k)] if isinstance(s, int) and s == 0 else wfull.at[strip(me - s, g, k)]
        return remote(
            src, wfull.at[strip(me - s, g, k)],
            right_send.at[s * chunks + k], right_recv.at[s * chunks + k], {"ctx": me + 1},
        )

    def go_left(s, k):
        src = w_ref.at[own_strip(k)] if isinstance(s, int) and s == 0 else wfull.at[strip(me + s, g, k)]
        return remote(
            src, wfull.at[strip(me + s, g, k)],
            left_send.at[s * chunks + k], left_recv.at[s * chunks + k], {"ctx": me - 1},
        )

    def arrival(s, k, from_left):
        at = strip(me - s if from_left else me + s, g, k)
        send, recv = (right_send, right_recv) if from_left else (left_send, left_recv)
        spot = (s - 1) * chunks + k
        return remote(
            wfull.at[at], wfull.at[at], send.at[spot], recv.at[spot], {"ctx": me}
        )

    def across(s, k, from_left, part):
        at = strip(me - s if from_left else me + s, part, k)
        send, recv = (yr_send, yr_recv) if from_left else (yl_send, yl_recv)
        spot = (s - 1) * chunks + k
        return remote(wfull.at[at], wfull.at[at], send.at[spot], recv.at[spot], {"groups": other})

    for k in range(chunks):

        @pl.when(has_right)
        def _():
            go_right(0, k).start()

        @pl.when(has_left)
        def _():
            go_left(0, k).start()

    own_copy = pltpu.make_async_copy(
        w_ref, wfull.at[pl.ds(pl.multiple_of(me * depth, 16), depth)], own_sem
    )
    own_copy.start()

    def relay(s, k):
        @pl.when(me - s >= 0)
        def _():
            arrival(s, k, True).wait_recv()

            @pl.when(has_right)
            def _():
                go_right(s, k).start()

            across(s, k, True, g).start()

        @pl.when(me + s < n)
        def _():
            arrival(s, k, False).wait_recv()

            @pl.when(has_left)
            def _():
                go_left(s, k).start()

            across(s, k, False, g).start()

    events = [(s, k) for s in range(1, min(n, 4)) for k in range(chunks)]

    def next_relay():
        if events:
            relay(*events.pop(0))

    @pl.when(jnp.logical_not(has_left))
    def _():
        halo_x[...] = jnp.zeros_like(halo_x)
        halo_b[...] = jnp.zeros_like(halo_b)
        halo_c[...] = jnp.zeros_like(halo_c)

    @pl.when(has_left)
    def _():
        for i in range(3):
            halo(i).wait_recv()

    def conv(src, rim, taps, dst, columns):
        xe[0:8] = rim[:, columns].astype(F32)[RIM - 8 :]
        xe[8 : 8 + rows] = src[:, columns].astype(F32)
        weights = taps(columns).astype(F32)
        for first in range(0, rows, 128):
            total = xe[first + 5 : first + 5 + 128] * weights[0:1]
            for tap in range(1, 4):
                total = total + xe[first + 5 + tap : first + 5 + tap + 128] * weights[tap : tap + 1]
            dst[first : first + 128, columns] = silu(total).astype(BF16)

    every = pl.ds(0, STATE)
    conv(b_ref, halo_b, lambda cols: convbc_ref[0, :, cols], bs, every)
    conv(c_ref, halo_c, lambda cols: convbc_ref[1, :, cols], cs, every)

    @pl.loop(0, inner // STATE)
    def _(tile):
        columns = pl.ds(pl.multiple_of(tile * STATE, STATE), STATE)
        conv(x_ref, halo_x, lambda cols: conv_ref[:, cols], xs, columns)

    raw = dt_ref[...].astype(F32) + bias_ref[...]
    step = jnp.maximum(raw, 0.0) + jnp.log1p(jnp.exp(-jnp.abs(raw)))
    log_decay = -jnp.exp(alog_ref[...]) * step
    t_at = lax.broadcasted_iota(jnp.int32, (SPAN, SPAN), 0)
    s_at = lax.broadcasted_iota(jnp.int32, (SPAN, SPAN), 1)
    causal = t_at >= s_at
    lower = causal.astype(F32)
    eye = (
        lax.broadcasted_iota(jnp.int32, (heads, heads), 0) == lax.broadcasted_iota(jnp.int32, (heads, heads), 1)
    ).astype(F32)

    def turned(value):
        return lax.dot_general(
            eye, value, (((1,), (1,)), ((), ())), precision=lax.Precision.HIGHEST, preferred_element_type=F32
        )

    def table(tile):
        channel = lax.broadcasted_iota(jnp.int32, (heads, TILE), 1) + tile * TILE
        first = lax.broadcasted_iota(jnp.int32, (heads, TILE), 0) * width
        return jnp.logical_and(channel >= first, channel < first + width).astype(BF16)

    tiles = inner // TILE
    tables = [table(tile) for tile in range(tiles)]
    states = (state0, state1)
    steps, cums, ends = [], [], []
    for span in range(spans):
        at = slice(span * SPAN, (span + 1) * SPAN)
        step_here = step[at]
        cum = jnp.dot(lower, log_decay[at], precision=lax.Precision.HIGHEST, preferred_element_type=F32)
        steps.append(step_here)
        cums.append(cum)
        to_end = jnp.exp(cum[SPAN - 1 : SPAN] - cum) * step_here
        b_turned = bs[at].astype(F32).T.astype(BF16)
        decay = []
        for tile in range(tiles):
            columns = slice(tile * TILE, (tile + 1) * TILE)
            weighted = (xs[at, columns].astype(F32) * spread(to_end, tables[tile])).astype(BF16)
            states[span][:, columns] = dot(b_turned, weighted)
            decay.append(spread(jnp.exp(cum[SPAN - 8 :]), tables[tile])[7:8])
        ends.append(decay)

    def hand_on():
        return remote(outgoing, entering, chain_send, chain_recv, {"ctx": me + 1})

    def pass_on(first):
        for tile in range(tiles):
            columns = slice(tile * TILE, (tile + 1) * TILE)
            total = ends[1][tile] * state0[:, columns] + state1[:, columns]
            if not first:
                total = total + ends[0][tile] * ends[1][tile] * entering[:, columns].astype(F32)
            outgoing[:, columns] = total.astype(BF16)
        hand_on().start()

    @pl.when(jnp.logical_not(has_left))
    def _():
        entering[...] = jnp.zeros_like(entering)
        pass_on(True)

    def chain_relay():
        hand_on().wait_recv()

        @pl.when(has_right)
        def _():
            pass_on(False)

    low_lane = lax.broadcasted_iota(jnp.int32, (128, 2 * width), 1) < width
    done = 0
    for span in range(spans):
        base = span * SPAN
        scores = lax.dot_general(
            cs[base : base + SPAN], bs[base : base + SPAN], (((1,), (1,)), ((), ())), preferred_element_type=F32
        )
        scores = jnp.where(causal, scores, 0.0)
        cum = cums[span]
        cum_turned = turned(cum)
        step_turned = turned(steps[span])
        for pair in range(heads // 2):
            columns = slice(pair * 2 * width, (pair + 1) * 2 * width)
            for block in range(2):
                top, reach = block * 128, (block + 1) * 128
                parts = []
                for head in (2 * pair, 2 * pair + 1):
                    gap = cum[top:reach, head : head + 1] - cum_turned[head : head + 1, :reach]
                    mixing = (
                        scores[top:reach, :reach] * jnp.exp(jnp.minimum(gap, 0.0))
                        * step_turned[head : head + 1, :reach]
                    ).astype(BF16)
                    parts.append(dot(mixing, xs[base : base + reach, columns]))
                ssd[base + top : base + reach, columns] = jnp.where(low_lane, parts[0], parts[1])
            done += 1
            if done in (4, 8, 12):

                @pl.when(me == done // 4)
                def _():
                    chain_relay()

            if done in (3, 11):
                next_relay()

    @pl.when(me > 3)
    def _():
        chain_relay()

    next_relay()

    blocks = lambda block, span: nall.at[block, pl.ds(span * SPAN, SPAN)]

    def to_near(span):
        return remote(blocks(p, span), blocks(p, span), tp_send.at[0, span], tp_recv.at[0, span], {"tp": near})

    def to_far(span):
        return remote(blocks(p, span), blocks(p, span), tp_send.at[1, span], tp_recv.at[1, span], {"tp": far})

    def far_to_near(span):
        return remote(blocks(far, span), blocks(far, span), tp_send.at[2, span], tp_recv.at[2, span], {"tp": near})

    skips = [spread(skip_ref[...] + jnp.zeros((8, heads), F32), tables[tile])[0:1] for tile in range(tiles)]
    for span in range(spans):
        at = slice(span * SPAN, (span + 1) * SPAN)
        growth = jnp.exp(cums[span])
        squares = jnp.zeros((SPAN, 1), F32)
        for tile in range(tiles):
            columns = slice(tile * TILE, (tile + 1) * TILE)
            held = entering[:, columns].astype(F32)
            if span == 0:
                carried = dot(cs[at], entering[:, columns])
            else:
                held = ends[0][tile] * held + state0[:, columns]
                high = held.astype(BF16)
                carried = dot(cs[at], high) + dot(cs[at], (held - high.astype(F32)).astype(BF16))
            full = ssd[at, columns] + carried * spread(growth, tables[tile])
            full = full + skips[tile] * xs[at, columns].astype(F32)
            gated = full * silu(z_ref[at, columns].astype(F32))
            ssd[at, columns] = gated
            squares = squares + jnp.sum(gated * gated, axis=1, keepdims=True)
        scale = lax.rsqrt(squares * (1.0 / inner) + EPS)
        for tile in range(tiles):
            columns = slice(tile * TILE, (tile + 1) * TILE)
            gain = gain_ref[:, columns].astype(F32)
            nall[p, at, columns] = (ssd[at, columns] * scale * gain).astype(BF16)
        to_far(span).start()
        to_near(span).start()

    next_relay()
    for span in range(spans):
        to_far(span).wait_recv()
        far_to_near(span).start()
    while events:
        next_relay()
    if n > 4:

        @pl.loop(4, n)
        def _(s):
            for k in range(chunks):
                relay(s, k)

    def settle(s, k):
        for from_left, go, there in ((True, go_right, me - s >= 0), (False, go_left, me + s < n)):

            @pl.when(there)
            def _():
                across(s, k, from_left, other).wait_recv()
                across(s, k, from_left, g).wait_send()

                @pl.when(has_right if from_left else has_left)
                def _():
                    go(s, k).wait_send()

    @pl.when(has_right)
    def _():
        hand_on().wait_send()
        for i in range(3):
            halo(i).wait_send()
        for k in range(chunks):
            go_right(0, k).wait_send()

    @pl.when(has_left)
    def _():
        for k in range(chunks):
            go_left(0, k).wait_send()

    own_copy.wait()
    for span in range(spans):
        to_near(span).wait_recv()
        far_to_near(span).wait_recv()
        to_near(span).wait_send()
        to_far(span).wait_send()
        far_to_near(span).wait_send()
    if n > 4:

        @pl.loop(1, n)
        def _(s):
            for k in range(chunks):
                settle(s, k)
    else:
        for s in range(1, n):
            for k in range(chunks):
                settle(s, k)

    @pl.loop(0, o_ref.shape[1] // TILE)
    def _(tile):
        columns = pl.ds(pl.multiple_of(tile * TILE, TILE), TILE)
        total = dot(nall[0], wfull[0:inner, columns])
        for block in range(1, 4):
            total = total + dot(nall[block], wfull[block * inner : (block + 1) * inner, columns])
        o_ref[:, columns] = total.astype(BF16)


def shards(
    x_in, z_in, b_in, c_in, dt_in, conv_x, conv_bc, dt_bias, a_log, d_skip, norm_gain, out_weight
):
    n = lax.axis_size("ctx")
    rows, inner = x_in.shape
    depth, out_columns = out_weight.shape
    assert lax.axis_size("tp") == 4 and lax.axis_size("groups") == 2
    assert b_in.shape[1] == STATE and rows == 2 * SPAN and conv_x.shape[0] == 4
    chunks = 2 if depth >= 256 else 1
    links = pltpu.SemaphoreType.DMA((n * chunks,))
    vmem = pl.BlockSpec(memory_space=pltpu.VMEM)
    return pl.pallas_call(
        functools.partial(kernel, n, chunks),
        out_shape=jax.ShapeDtypeStruct((rows, out_columns), BF16),
        in_specs=[vmem] * 11 + [pl.BlockSpec(memory_space=pl.ANY)],
        out_specs=vmem,
        scratch_shapes=[
            pltpu.VMEM((n * depth, out_columns), BF16),
            pltpu.VMEM((4, rows, inner), BF16),
            pltpu.VMEM((rows + 8, STATE), F32),
            pltpu.VMEM((rows, inner), BF16),
            pltpu.VMEM((rows, STATE), BF16),
            pltpu.VMEM((rows, STATE), BF16),
            pltpu.VMEM((rows, inner), F32),
            pltpu.VMEM((STATE, inner), F32),
            pltpu.VMEM((STATE, inner), F32),
            pltpu.VMEM((STATE, inner), BF16),
            pltpu.VMEM((STATE, inner), BF16),
            pltpu.VMEM((RIM, inner), BF16),
            pltpu.VMEM((RIM, STATE), BF16),
            pltpu.VMEM((RIM, STATE), BF16),
            pltpu.SemaphoreType.DMA,
            pltpu.SemaphoreType.DMA((3,)),
            pltpu.SemaphoreType.DMA((3,)),
            pltpu.SemaphoreType.DMA,
            pltpu.SemaphoreType.DMA,
        ]
        + [links] * 8
        + [pltpu.SemaphoreType.DMA((3, 2)), pltpu.SemaphoreType.DMA((3, 2))],
        compiler_params=pltpu.CompilerParams(
            collective_id=0, has_side_effects=True, vmem_limit_bytes=48 * 1024 * 1024
        ),
    )(
        x_in, z_in, b_in, c_in, dt_in, conv_x, conv_bc,
        dt_bias[None], a_log[None], d_skip[None], norm_gain[None], out_weight,
    )


def solution(mesh):
    rows = P(("groups", "ctx"), "tp")
    return jax.shard_map(
        shards,
        mesh=mesh,
        in_specs=(
            rows, rows, rows, rows, rows,
            P(None, "tp"), P(None, None, "tp"),
            P("tp"), P("tp"), P("tp"), P("tp"),
            P("ctx", "tp"),
        ),
        out_specs=rows,
        check_vma=False,
    )
```

```python
import functools
import jax
import jax.numpy as jnp
from jax import lax
from jax.experimental import pallas as pl
from jax.experimental.pallas import tpu as pltpu
from jax.sharding import PartitionSpec as P

STATE = 128
SPAN = 256
EPS = 1e-05
RIM = 16
TILE = 256
MESH = pl.DeviceIdType.MESH
F32 = jnp.float32
BF16 = jnp.bfloat16


def dot(a, b):
    return jnp.dot(a, b, preferred_element_type=F32)


def silu(v):
    return v / (1.0 + jnp.exp(-v))


def spread(value, table):
    high = value.astype(BF16)
    low = (value - high.astype(F32)).astype(BF16)
    return dot(high, table) + dot(low, table)


def kernel(
    n, chunks,
    x_hbm, z_hbm, b_hbm, c_hbm, dt_hbm, conv_hbm, convbc_hbm, bias_hbm, alog_hbm, skip_hbm, gain_hbm, w_ref,
    o_ref,
    x_ref, z_ref, b_ref, c_ref, dt_ref, conv_ref, convbc_ref, bias_ref, alog_ref, skip_ref, gain_ref, in_sem, total_ref,
    wfull, nall, xe, xs, bs, cs, ssd, state0, state1, entering, outgoing, halo_x, halo_b, halo_c,
    own_sem, halo_send, halo_recv, chain_send, chain_recv,
    right_send, right_recv, left_send, left_recv,
    yr_send, yr_recv, yl_send, yl_recv,
    tp_send, tp_recv,
):
    g = lax.axis_index("groups")
    me = lax.axis_index("ctx")
    p = lax.axis_index("tp")
    other = 1 - g
    near = p + 1 - 2 * lax.rem(p, 2)
    far = lax.rem(p + 2, 4)
    rows, inner = x_ref.shape
    heads = dt_ref.shape[1]
    width = inner // heads
    spans = rows // SPAN
    depth = w_ref.shape[0]
    half = depth // 2
    piece = half // chunks
    has_left, has_right = me > 0, me < n - 1

    sources = (x_hbm, z_hbm, b_hbm, c_hbm, dt_hbm, conv_hbm, convbc_hbm, bias_hbm, alog_hbm, skip_hbm, gain_hbm)
    held_in = (x_ref, z_ref, b_ref, c_ref, dt_ref, conv_ref, convbc_ref, bias_ref, alog_ref, skip_ref, gain_ref)
    loads = [
        pltpu.make_async_copy(source, to, in_sem.at[i]) for i, (source, to) in enumerate(zip(sources, held_in))
    ]
    barrier = pltpu.get_barrier_semaphore()
    for device in ({"groups": other}, {"tp": near}, {"tp": far}):
        pl.semaphore_signal(barrier, inc=1, device_id=device, device_id_type=MESH)

    @pl.when(has_left)
    def _():
        pl.semaphore_signal(barrier, inc=1, device_id={"ctx": me - 1}, device_id_type=MESH)

    @pl.when(has_right)
    def _():
        pl.semaphore_signal(barrier, inc=1, device_id={"ctx": me + 1}, device_id_type=MESH)

    for load in loads:
        load.start()
    pl.semaphore_wait(barrier, 3 + has_left.astype(jnp.int32) + has_right.astype(jnp.int32))

    def remote(src, dst, send, recv, device):
        return pltpu.make_async_remote_copy(
            src_ref=src, dst_ref=dst, send_sem=send, recv_sem=recv, device_id=device, device_id_type=MESH
        )

    def halo(i):
        src = (x_hbm, b_hbm, c_hbm)[i].at[pl.ds(rows - RIM, RIM)]
        dst = (halo_x, halo_b, halo_c)[i]
        return remote(src, dst, halo_send.at[i], halo_recv.at[i], {"ctx": me + 1})

    @pl.when(has_right)
    def _():
        for i in range(3):
            halo(i).start()

    def strip(block, part, k):
        return pl.ds(pl.multiple_of(block * depth + part * half + k * piece, 16), piece)

    def own_strip(k):
        return pl.ds(pl.multiple_of(g * half + k * piece, 16), piece)

    def go_right(s, k):
        src = w_ref.at[own_strip(k)] if isinstance(s, int) and s == 0 else wfull.at[strip(me - s, g, k)]
        return remote(
            src, wfull.at[strip(me - s, g, k)],
            right_send.at[s * chunks + k], right_recv.at[s * chunks + k], {"ctx": me + 1},
        )

    def go_left(s, k):
        src = w_ref.at[own_strip(k)] if isinstance(s, int) and s == 0 else wfull.at[strip(me + s, g, k)]
        return remote(
            src, wfull.at[strip(me + s, g, k)],
            left_send.at[s * chunks + k], left_recv.at[s * chunks + k], {"ctx": me - 1},
        )

    def arrival(s, k, from_left):
        at = strip(me - s if from_left else me + s, g, k)
        send, recv = (right_send, right_recv) if from_left else (left_send, left_recv)
        spot = (s - 1) * chunks + k
        return remote(
            wfull.at[at], wfull.at[at], send.at[spot], recv.at[spot], {"ctx": me}
        )

    def across(s, k, from_left, part):
        at = strip(me - s if from_left else me + s, part, k)
        send, recv = (yr_send, yr_recv) if from_left else (yl_send, yl_recv)
        spot = (s - 1) * chunks + k
        return remote(wfull.at[at], wfull.at[at], send.at[spot], recv.at[spot], {"groups": other})

    for k in range(chunks):

        @pl.when(has_right)
        def _():
            go_right(0, k).start()

        @pl.when(has_left)
        def _():
            go_left(0, k).start()

    own_copy = pltpu.make_async_copy(
        w_ref, wfull.at[pl.ds(pl.multiple_of(me * depth, 16), depth)], own_sem
    )
    own_copy.start()

    def relay(s, k):
        @pl.when(me - s >= 0)
        def _():
            arrival(s, k, True).wait_recv()

            @pl.when(has_right)
            def _():
                go_right(s, k).start()

            across(s, k, True, g).start()

        @pl.when(me + s < n)
        def _():
            arrival(s, k, False).wait_recv()

            @pl.when(has_left)
            def _():
                go_left(s, k).start()

            across(s, k, False, g).start()

    events = [(s, k) for s in range(1, min(n, 4)) for k in range(chunks)]

    def next_relay():
        if events:
            relay(*events.pop(0))

    for i in (2, 3, 0, 4, 5, 6, 7, 8):
        loads[i].wait()

    @pl.when(jnp.logical_not(has_left))
    def _():
        halo_x[...] = jnp.zeros_like(halo_x)
        halo_b[...] = jnp.zeros_like(halo_b)
        halo_c[...] = jnp.zeros_like(halo_c)

    @pl.when(has_left)
    def _():
        for i in range(3):
            halo(i).wait_recv()

    def conv(src, rim, taps, dst, columns):
        xe[0:8] = rim[:, columns].astype(F32)[RIM - 8 :]
        xe[8 : 8 + rows] = src[:, columns].astype(F32)
        weights = taps(columns).astype(F32)
        for first in range(0, rows, 128):
            total = xe[first + 5 : first + 5 + 128] * weights[0:1]
            for tap in range(1, 4):
                total = total + xe[first + 5 + tap : first + 5 + tap + 128] * weights[tap : tap + 1]
            dst[first : first + 128, columns] = silu(total).astype(BF16)

    every = pl.ds(0, STATE)
    conv(b_ref, halo_b, lambda cols: convbc_ref[0, :, cols], bs, every)
    conv(c_ref, halo_c, lambda cols: convbc_ref[1, :, cols], cs, every)

    @pl.loop(0, inner // STATE)
    def _(tile):
        columns = pl.ds(pl.multiple_of(tile * STATE, STATE), STATE)
        conv(x_ref, halo_x, lambda cols: conv_ref[:, cols], xs, columns)

    raw = dt_ref[...].astype(F32) + bias_ref[...]
    step = jnp.maximum(raw, 0.0) + jnp.log1p(jnp.exp(-jnp.abs(raw)))
    log_decay = -jnp.exp(alog_ref[...]) * step
    t_at = lax.broadcasted_iota(jnp.int32, (SPAN, SPAN), 0)
    s_at = lax.broadcasted_iota(jnp.int32, (SPAN, SPAN), 1)
    causal = t_at >= s_at
    lower = causal.astype(F32)
    eye = (
        lax.broadcasted_iota(jnp.int32, (heads, heads), 0) == lax.broadcasted_iota(jnp.int32, (heads, heads), 1)
    ).astype(F32)

    def turned(value):
        return lax.dot_general(
            eye, value, (((1,), (1,)), ((), ())), precision=lax.Precision.HIGHEST, preferred_element_type=F32
        )

    def table(tile):
        channel = lax.broadcasted_iota(jnp.int32, (heads, TILE), 1) + tile * TILE
        first = lax.broadcasted_iota(jnp.int32, (heads, TILE), 0) * width
        return jnp.logical_and(channel >= first, channel < first + width).astype(BF16)

    tiles = inner // TILE
    tables = [table(tile) for tile in range(tiles)]
    states = (state0, state1)
    steps, cums, ends = [], [], []
    for span in range(spans):
        at = slice(span * SPAN, (span + 1) * SPAN)
        step_here = step[at]
        cum = jnp.dot(lower, log_decay[at], precision=lax.Precision.HIGHEST, preferred_element_type=F32)
        steps.append(step_here)
        cums.append(cum)
        to_end = jnp.exp(cum[SPAN - 1 : SPAN] - cum) * step_here
        b_turned = bs[at].astype(F32).T.astype(BF16)
        decay = []
        for tile in range(tiles):
            columns = slice(tile * TILE, (tile + 1) * TILE)
            weighted = (xs[at, columns].astype(F32) * spread(to_end, tables[tile])).astype(BF16)
            states[span][:, columns] = dot(b_turned, weighted)
            decay.append(spread(jnp.exp(cum[SPAN - 8 :]), tables[tile])[7:8])
        ends.append(decay)

    def hand_on(tile):
        return remote(
            outgoing.at[tile], entering.at[tile], chain_send.at[tile], chain_recv.at[tile], {"ctx": me + 1}
        )

    def pass_on(tile, first):
        columns = slice(tile * TILE, (tile + 1) * TILE)
        total = ends[1][tile] * state0[:, columns] + state1[:, columns]
        if not first:
            total = total + ends[0][tile] * ends[1][tile] * entering[tile].astype(F32)
        outgoing[tile] = total.astype(BF16)
        hand_on(tile).start()

    @pl.when(jnp.logical_not(has_left))
    def _():
        entering[...] = jnp.zeros_like(entering)
        for tile in range(tiles):
            pass_on(tile, True)

    def chain_relay(tile):
        @pl.when(has_left)
        def _():
            hand_on(tile).wait_recv()

            @pl.when(has_right)
            def _():
                pass_on(tile, False)

    low_lane = lax.broadcasted_iota(jnp.int32, (128, 2 * width), 1) < width
    done = 0
    for span in range(spans):
        base = span * SPAN
        scores = lax.dot_general(
            cs[base : base + SPAN], bs[base : base + SPAN], (((1,), (1,)), ((), ())), preferred_element_type=F32
        )
        scores = jnp.where(causal, scores, 0.0)
        cum = cums[span]
        cum_turned = turned(cum)
        step_turned = turned(steps[span])
        for pair in range(heads // 2):
            columns = slice(pair * 2 * width, (pair + 1) * 2 * width)
            for block in range(2):
                top, reach = block * 128, (block + 1) * 128
                parts = []
                for head in (2 * pair, 2 * pair + 1):
                    gap = cum[top:reach, head : head + 1] - cum_turned[head : head + 1, :reach]
                    mixing = (
                        scores[top:reach, :reach] * jnp.exp(jnp.minimum(gap, 0.0))
                        * step_turned[head : head + 1, :reach]
                    ).astype(BF16)
                    parts.append(dot(mixing, xs[base : base + reach, columns]))
                ssd[base + top : base + reach, columns] = jnp.where(low_lane, parts[0], parts[1])
            done += 1
            if done == 8:
                next_relay()

    next_relay()
    for tile in range(tiles):
        chain_relay(tile)
        if tile in (1, 2):
            next_relay()

    loads[1].wait()
    loads[9].wait()
    loads[10].wait()

    blocks = lambda block, span: nall.at[block, pl.ds(span * SPAN, SPAN)]

    def to_near(span):
        return remote(blocks(p, span), blocks(p, span), tp_send.at[0, span], tp_recv.at[0, span], {"tp": near})

    def to_far(span):
        return remote(blocks(p, span), blocks(p, span), tp_send.at[1, span], tp_recv.at[1, span], {"tp": far})

    def far_to_near(span):
        return remote(blocks(far, span), blocks(far, span), tp_send.at[2, span], tp_recv.at[2, span], {"tp": near})

    skips = [spread(skip_ref[...] + jnp.zeros((8, heads), F32), tables[tile])[0:1] for tile in range(tiles)]
    for span in range(spans):
        at = slice(span * SPAN, (span + 1) * SPAN)
        growth = jnp.exp(cums[span])
        squares = jnp.zeros((SPAN, 1), F32)
        for tile in range(tiles):
            columns = slice(tile * TILE, (tile + 1) * TILE)
            held = entering[tile].astype(F32)
            if span == 0:
                carried = dot(cs[at], entering[tile])
            else:
                held = ends[0][tile] * held + state0[:, columns]
                high = held.astype(BF16)
                carried = dot(cs[at], high) + dot(cs[at], (held - high.astype(F32)).astype(BF16))
            full = ssd[at, columns] + carried * spread(growth, tables[tile])
            full = full + skips[tile] * xs[at, columns].astype(F32)
            gated = full * silu(z_ref[at, columns].astype(F32))
            ssd[at, columns] = gated
            squares = squares + jnp.sum(gated * gated, axis=1, keepdims=True)
        scale = lax.rsqrt(squares * (1.0 / inner) + EPS)
        for tile in range(tiles):
            columns = slice(tile * TILE, (tile + 1) * TILE)
            gain = gain_ref[:, columns].astype(F32)
            nall[p, at, columns] = (ssd[at, columns] * scale * gain).astype(BF16)
        to_far(span).start()
        to_near(span).start()

    def settle(s, k):
        for from_left, there in ((True, me - s >= 0), (False, me + s < n)):

            @pl.when(there)
            def _():
                across(s, k, from_left, other).wait_recv()

    def gathered(span):
        to_near(span).wait_recv()
        far_to_near(span).wait_recv()

    def multiply(block, first=False):
        @pl.loop(0, o_ref.shape[1] // TILE)
        def _(tile):
            columns = pl.ds(pl.multiple_of(tile * TILE, TILE), TILE)
            part = dot(nall[block], wfull[pl.ds(pl.multiple_of(block * depth, 16), depth), columns])
            if first:
                total_ref[:, columns] = part
            else:
                total_ref[:, columns] += part

    def multiply_around(s):
        for k in range(chunks):
            settle(s, k)

        @pl.when(me - s >= 0)
        def _():
            multiply(me - s)

        @pl.when(me + s < n)
        def _():
            multiply(me + s)

    def relays(count):
        for _ in range(count):
            next_relay()

    stepwise = depth == inner
    relays(2)
    to_far(0).wait_recv()
    far_to_near(0).start()
    relays(3)
    to_far(1).wait_recv()
    far_to_near(1).start()
    own_copy.wait()
    relays(1)
    for span in range(spans):
        gathered(span)
    if stepwise:
        multiply(me, True)
        multiply_around(1)
        for s in range(2, n):
            while events and events[0][0] <= s:
                next_relay()
            multiply_around(s)
    else:
        while events:
            next_relay()

        @pl.loop(4, n)
        def _(s):
            for k in range(chunks):
                relay(s, k)

        @pl.loop(1, n)
        def _(s):
            for k in range(chunks):
                settle(s, k)

    def sent(s, k):
        for from_left, go, there in ((True, go_right, me - s >= 0), (False, go_left, me + s < n)):

            @pl.when(there)
            def _():
                across(s, k, from_left, g).wait_send()

                @pl.when(has_right if from_left else has_left)
                def _():
                    go(s, k).wait_send()

    @pl.when(has_right)
    def _():
        for tile in range(tiles):
            hand_on(tile).wait_send()
        for i in range(3):
            halo(i).wait_send()
        for k in range(chunks):
            go_right(0, k).wait_send()

    @pl.when(has_left)
    def _():
        for k in range(chunks):
            go_left(0, k).wait_send()

    for span in range(spans):
        to_near(span).wait_send()
        to_far(span).wait_send()
        far_to_near(span).wait_send()
    if n > 4:

        @pl.loop(1, n)
        def _(s):
            for k in range(chunks):
                sent(s, k)
    else:
        for s in range(1, n):
            for k in range(chunks):
                sent(s, k)

    @pl.loop(0, o_ref.shape[1] // TILE)
    def _(tile):
        columns = pl.ds(pl.multiple_of(tile * TILE, TILE), TILE)
        if stepwise:
            o_ref[:, columns] = total_ref[:, columns].astype(BF16)
        else:
            total = dot(nall[0], wfull[0:inner, columns])
            for block in range(1, 4):
                total = total + dot(nall[block], wfull[block * inner : (block + 1) * inner, columns])
            o_ref[:, columns] = total.astype(BF16)


def shards(
    x_in, z_in, b_in, c_in, dt_in, conv_x, conv_bc, dt_bias, a_log, d_skip, norm_gain, out_weight
):
    n = lax.axis_size("ctx")
    rows, inner = x_in.shape
    depth, out_columns = out_weight.shape
    assert lax.axis_size("tp") == 4 and lax.axis_size("groups") == 2
    assert b_in.shape[1] == STATE and rows == 2 * SPAN and conv_x.shape[0] == 4
    chunks = 4 if depth >= 256 else 1
    links = pltpu.SemaphoreType.DMA((n * chunks,))
    vmem = pl.BlockSpec(memory_space=pltpu.VMEM)
    operands = (
        x_in, z_in, b_in, c_in, dt_in, conv_x, conv_bc,
        dt_bias[None], a_log[None], d_skip[None], norm_gain[None],
    )
    return pl.pallas_call(
        functools.partial(kernel, n, chunks),
        out_shape=jax.ShapeDtypeStruct((rows, out_columns), BF16),
        in_specs=[pl.BlockSpec(memory_space=pl.ANY)] * 12,
        out_specs=vmem,
        scratch_shapes=[pltpu.VMEM(operand.shape, operand.dtype) for operand in operands]
        + [pltpu.SemaphoreType.DMA((len(operands),)), pltpu.VMEM((rows, out_columns), F32)]
        + [
            pltpu.VMEM((n * depth, out_columns), BF16),
            pltpu.VMEM((4, rows, inner), BF16),
            pltpu.VMEM((rows + 8, STATE), F32),
            pltpu.VMEM((rows, inner), BF16),
            pltpu.VMEM((rows, STATE), BF16),
            pltpu.VMEM((rows, STATE), BF16),
            pltpu.VMEM((rows, inner), F32),
            pltpu.VMEM((STATE, inner), F32),
            pltpu.VMEM((STATE, inner), F32),
            pltpu.VMEM((inner // TILE, STATE, TILE), BF16),
            pltpu.VMEM((inner // TILE, STATE, TILE), BF16),
            pltpu.VMEM((RIM, inner), BF16),
            pltpu.VMEM((RIM, STATE), BF16),
            pltpu.VMEM((RIM, STATE), BF16),
            pltpu.SemaphoreType.DMA,
            pltpu.SemaphoreType.DMA((3,)),
            pltpu.SemaphoreType.DMA((3,)),
            pltpu.SemaphoreType.DMA((inner // TILE,)),
            pltpu.SemaphoreType.DMA((inner // TILE,)),
        ]
        + [links] * 8
        + [pltpu.SemaphoreType.DMA((3, 2)), pltpu.SemaphoreType.DMA((3, 2))],
        compiler_params=pltpu.CompilerParams(
            collective_id=0, has_side_effects=True, vmem_limit_bytes=48 * 1024 * 1024
        ),
    )(*operands, out_weight)


def solution(mesh):
    rows = P(("groups", "ctx"), "tp")
    return jax.shard_map(
        shards,
        mesh=mesh,
        in_specs=(
            rows, rows, rows, rows, rows,
            P(None, "tp"), P(None, None, "tp"),
            P("tp"), P("tp"), P("tp"), P("tp"),
            P("ctx", "tp"),
        ),
        out_specs=rows,
        check_vma=False,
    )
```

```python
import functools
import jax
import jax.numpy as jnp
from jax import lax
from jax.experimental import pallas as pl
from jax.experimental.pallas import tpu as pltpu
from jax.sharding import PartitionSpec as P

STATE = 128
SPAN = 256
EPS = 1e-05
RIM = 16
TILE = 256
MESH = pl.DeviceIdType.MESH
F32 = jnp.float32
BF16 = jnp.bfloat16


def dot(a, b):
    return jnp.dot(a, b, preferred_element_type=F32)


def silu(v):
    return v / (1.0 + jnp.exp(-v))


def spread(value, table):
    high = value.astype(BF16)
    low = (value - high.astype(F32)).astype(BF16)
    return dot(high, table) + dot(low, table)


def kernel(
    n, chunks,
    x_hbm, z_hbm, b_hbm, c_hbm, dt_hbm, conv_hbm, convbc_hbm, bias_hbm, alog_hbm, skip_hbm, gain_hbm, w_ref,
    o_ref,
    x_ref, z_ref, b_ref, c_ref, dt_ref, conv_ref, convbc_ref, bias_ref, alog_ref, skip_ref, gain_ref, in_sem, total_ref,
    wfull, nall, xe, xs, bs, cs, ssd, state0, state1, entering, outgoing, halo_x, halo_b, halo_c,
    own_sem, halo_send, halo_recv, chain_send, chain_recv,
    right_send, right_recv, left_send, left_recv,
    yr_send, yr_recv, yl_send, yl_recv,
    tp_send, tp_recv,
):
    g = lax.axis_index("groups")
    me = lax.axis_index("ctx")
    p = lax.axis_index("tp")
    other = 1 - g
    near = p + 1 - 2 * lax.rem(p, 2)
    far = lax.rem(p + 2, 4)
    rows, inner = x_ref.shape
    heads = dt_ref.shape[0]
    width = inner // heads
    spans = rows // SPAN
    depth = w_ref.shape[0]
    half = depth // 2
    piece = half // chunks
    has_left, has_right = me > 0, me < n - 1

    sources = (x_hbm, z_hbm, b_hbm, c_hbm, dt_hbm, conv_hbm, convbc_hbm, bias_hbm, alog_hbm, skip_hbm, gain_hbm)
    held_in = (x_ref, z_ref, b_ref, c_ref, dt_ref, conv_ref, convbc_ref, bias_ref, alog_ref, skip_ref, gain_ref)
    loads = [
        pltpu.make_async_copy(source, to, in_sem.at[i]) for i, (source, to) in enumerate(zip(sources, held_in))
    ]
    barrier = pltpu.get_barrier_semaphore()
    for device in ({"groups": other}, {"tp": near}, {"tp": far}):
        pl.semaphore_signal(barrier, inc=1, device_id=device, device_id_type=MESH)

    @pl.when(has_left)
    def _():
        pl.semaphore_signal(barrier, inc=1, device_id={"ctx": me - 1}, device_id_type=MESH)

    @pl.when(has_right)
    def _():
        pl.semaphore_signal(barrier, inc=1, device_id={"ctx": me + 1}, device_id_type=MESH)

    for load in loads:
        load.start()
    pl.semaphore_wait(barrier, 3 + has_left.astype(jnp.int32) + has_right.astype(jnp.int32))

    def remote(src, dst, send, recv, device):
        return pltpu.make_async_remote_copy(
            src_ref=src, dst_ref=dst, send_sem=send, recv_sem=recv, device_id=device, device_id_type=MESH
        )

    def halo(i):
        src = (x_hbm, b_hbm, c_hbm)[i].at[pl.ds(rows - RIM, RIM)]
        dst = (halo_x, halo_b, halo_c)[i]
        return remote(src, dst, halo_send.at[i], halo_recv.at[i], {"ctx": me + 1})

    @pl.when(has_right)
    def _():
        for i in range(3):
            halo(i).start()

    def strip(block, part, k):
        return pl.ds(pl.multiple_of(block * depth + part * half + k * piece, 16), piece)

    def own_strip(k):
        return pl.ds(pl.multiple_of(g * half + k * piece, 16), piece)

    def go_right(s, k):
        src = w_ref.at[own_strip(k)] if isinstance(s, int) and s == 0 else wfull.at[strip(me - s, g, k)]
        return remote(
            src, wfull.at[strip(me - s, g, k)],
            right_send.at[s * chunks + k], right_recv.at[s * chunks + k], {"ctx": me + 1},
        )

    def go_left(s, k):
        src = w_ref.at[own_strip(k)] if isinstance(s, int) and s == 0 else wfull.at[strip(me + s, g, k)]
        return remote(
            src, wfull.at[strip(me + s, g, k)],
            left_send.at[s * chunks + k], left_recv.at[s * chunks + k], {"ctx": me - 1},
        )

    def arrival(s, k, from_left):
        at = strip(me - s if from_left else me + s, g, k)
        send, recv = (right_send, right_recv) if from_left else (left_send, left_recv)
        spot = (s - 1) * chunks + k
        return remote(
            wfull.at[at], wfull.at[at], send.at[spot], recv.at[spot], {"ctx": me}
        )

    def across(s, k, from_left, part):
        at = strip(me - s if from_left else me + s, part, k)
        send, recv = (yr_send, yr_recv) if from_left else (yl_send, yl_recv)
        spot = (s - 1) * chunks + k
        return remote(wfull.at[at], wfull.at[at], send.at[spot], recv.at[spot], {"groups": other})

    early = min(2, chunks)
    for k in range(chunks):
        if k < early:

            @pl.when(has_right)
            def _():
                go_right(0, k).start()

        @pl.when(has_left)
        def _():
            go_left(0, k).start()

    own_copy = pltpu.make_async_copy(
        w_ref, wfull.at[pl.ds(pl.multiple_of(me * depth, 16), depth)], own_sem
    )
    own_copy.start()

    def onward(s, k):
        @pl.when(jnp.logical_and(me - s >= 0, has_right))
        def _():
            go_right(s, k).start()

    def relay(s, k, hold=False):
        @pl.when(me + s < n)
        def _():
            arrival(s, k, False).wait_recv()

            @pl.when(has_left)
            def _():
                go_left(s, k).start()

            across(s, k, False, g).start()

        @pl.when(me - s >= 0)
        def _():
            arrival(s, k, True).wait_recv()
            across(s, k, True, g).start()

        if not hold:
            onward(s, k)

    events = [(s, k) for s in range(1, min(n, 4)) for k in range(chunks)]

    held_back = []

    def next_relay(hold=False):
        if events:
            if hold:
                held_back.append(events[0])
            relay(*events.pop(0), hold)

    for i in (2, 3, 0, 4, 5, 6, 7, 8):
        loads[i].wait()

    @pl.when(jnp.logical_not(has_left))
    def _():
        halo_x[...] = jnp.zeros_like(halo_x)
        halo_b[...] = jnp.zeros_like(halo_b)
        halo_c[...] = jnp.zeros_like(halo_c)

    @pl.when(has_left)
    def _():
        for i in range(3):
            halo(i).wait_recv()

    def conv(src, rim, taps, dst, columns):
        xe[0:8] = rim[:, columns].astype(F32)[RIM - 8 :]
        xe[8 : 8 + rows] = src[:, columns].astype(F32)
        weights = taps(columns).astype(F32)
        for first in range(0, rows, 128):
            total = xe[first + 5 : first + 5 + 128] * weights[0:1]
            for tap in range(1, 4):
                total = total + xe[first + 5 + tap : first + 5 + tap + 128] * weights[tap : tap + 1]
            dst[first : first + 128, columns] = silu(total).astype(BF16)

    every = pl.ds(0, STATE)
    conv(b_ref, halo_b, lambda cols: convbc_ref[0, :, cols], bs, every)
    conv(c_ref, halo_c, lambda cols: convbc_ref[1, :, cols], cs, every)

    @pl.loop(0, inner // STATE)
    def _(tile):
        columns = pl.ds(pl.multiple_of(tile * STATE, STATE), STATE)
        conv(x_ref, halo_x, lambda cols: conv_ref[:, cols], xs, columns)

    raw = dt_ref[...].astype(F32).T + bias_ref[...]
    step = jnp.maximum(raw, 0.0) + jnp.log1p(jnp.exp(-jnp.abs(raw)))
    log_decay = -jnp.exp(alog_ref[...]) * step
    t_at = lax.broadcasted_iota(jnp.int32, (SPAN, SPAN), 0)
    s_at = lax.broadcasted_iota(jnp.int32, (SPAN, SPAN), 1)
    causal = t_at >= s_at
    lower = causal.astype(F32)
    eye = (
        lax.broadcasted_iota(jnp.int32, (heads, heads), 0) == lax.broadcasted_iota(jnp.int32, (heads, heads), 1)
    ).astype(F32)

    def turned(value):
        return lax.dot_general(
            eye, value, (((1,), (1,)), ((), ())), precision=lax.Precision.HIGHEST, preferred_element_type=F32
        )

    def table(tile):
        channel = lax.broadcasted_iota(jnp.int32, (heads, TILE), 1) + tile * TILE
        first = lax.broadcasted_iota(jnp.int32, (heads, TILE), 0) * width
        return jnp.logical_and(channel >= first, channel < first + width).astype(BF16)

    tiles = inner // TILE
    tables = [table(tile) for tile in range(tiles)]
    states = (state0, state1)
    steps, cums, ends = [], [], []
    for span in range(spans):
        at = slice(span * SPAN, (span + 1) * SPAN)
        step_here = step[at]
        cum = jnp.dot(lower, log_decay[at], precision=lax.Precision.HIGHEST, preferred_element_type=F32)
        steps.append(step_here)
        cums.append(cum)
        to_end = jnp.exp(cum[SPAN - 1 : SPAN] - cum) * step_here
        b_turned = bs[at].astype(F32).T.astype(BF16)
        decay = []
        for tile in range(tiles):
            columns = slice(tile * TILE, (tile + 1) * TILE)
            weighted = (xs[at, columns].astype(F32) * spread(to_end, tables[tile])).astype(BF16)
            states[span][:, columns] = dot(b_turned, weighted)
            decay.append(spread(jnp.exp(cum[SPAN - 8 :]), tables[tile])[7:8])
        ends.append(decay)

    def hand_on(tile):
        return remote(
            outgoing.at[tile], entering.at[tile], chain_send.at[tile], chain_recv.at[tile], {"ctx": me + 1}
        )

    def pass_on(tile, first):
        columns = slice(tile * TILE, (tile + 1) * TILE)
        total = ends[1][tile] * state0[:, columns] + state1[:, columns]
        if not first:
            total = total + ends[0][tile] * ends[1][tile] * entering[tile].astype(F32)
        outgoing[tile] = total.astype(BF16)
        hand_on(tile).start()

    @pl.when(jnp.logical_not(has_left))
    def _():
        entering[...] = jnp.zeros_like(entering)
        for tile in range(tiles):
            pass_on(tile, True)

    def chain_relay(tile):
        @pl.when(has_left)
        def _():
            hand_on(tile).wait_recv()

            @pl.when(has_right)
            def _():
                pass_on(tile, False)

    low_lane = lax.broadcasted_iota(jnp.int32, (128, 2 * width), 1) < width
    done = 0
    for span in range(spans):
        base = span * SPAN
        scores = lax.dot_general(
            cs[base : base + SPAN], bs[base : base + SPAN], (((1,), (1,)), ((), ())), preferred_element_type=F32
        )
        scores = jnp.where(causal, scores, 0.0)
        cum = cums[span]
        cum_turned = turned(cum)
        step_turned = turned(steps[span])
        for pair in range(heads // 2):
            columns = slice(pair * 2 * width, (pair + 1) * 2 * width)
            for block in range(2):
                top, reach = block * 128, (block + 1) * 128
                parts = []
                for head in (2 * pair, 2 * pair + 1):
                    gap = cum[top:reach, head : head + 1] - cum_turned[head : head + 1, :reach]
                    mixing = (
                        scores[top:reach, :reach] * jnp.exp(jnp.minimum(gap, 0.0))
                        * step_turned[head : head + 1, :reach]
                    ).astype(BF16)
                    parts.append(dot(mixing, xs[base : base + reach, columns]))
                ssd[base + top : base + reach, columns] = jnp.where(low_lane, parts[0], parts[1])
            done += 1
            if done == 12 and early > 1:
                next_relay(True)

    for tile in range(tiles):
        chain_relay(tile)
    for k in range(early, chunks):

        @pl.when(has_right)
        def _():
            go_right(0, k).start()

    for s, k in held_back:
        onward(s, k)
    next_relay()

    loads[1].wait()
    loads[9].wait()
    loads[10].wait()

    blocks = lambda block, span: nall.at[block, pl.ds(span * SPAN, SPAN)]

    def to_near(span):
        return remote(blocks(p, span), blocks(p, span), tp_send.at[0, span], tp_recv.at[0, span], {"tp": near})

    def to_far(span):
        return remote(blocks(p, span), blocks(p, span), tp_send.at[1, span], tp_recv.at[1, span], {"tp": far})

    def far_to_near(span):
        return remote(blocks(far, span), blocks(far, span), tp_send.at[2, span], tp_recv.at[2, span], {"tp": near})

    gains, per = gain_ref[...].astype(F32), TILE // 128
    skips = [spread(skip_ref[...] + jnp.zeros((8, heads), F32), tables[tile])[0:1] for tile in range(tiles)]
    for span in range(spans):
        at = slice(span * SPAN, (span + 1) * SPAN)
        growth = jnp.exp(cums[span])
        squares = jnp.zeros((SPAN, 1), F32)
        for tile in range(tiles):
            columns = slice(tile * TILE, (tile + 1) * TILE)
            held = entering[tile].astype(F32)
            if span == 0:
                carried = dot(cs[at], entering[tile])
            else:
                held = ends[0][tile] * held + state0[:, columns]
                high = held.astype(BF16)
                carried = dot(cs[at], high) + dot(cs[at], (held - high.astype(F32)).astype(BF16))
            full = ssd[at, columns] + carried * spread(growth, tables[tile])
            full = full + skips[tile] * xs[at, columns].astype(F32)
            gated = full * silu(z_ref[at, columns].astype(F32))
            ssd[at, columns] = gated
            squares = squares + jnp.sum(gated * gated, axis=1, keepdims=True)
        scale = lax.rsqrt(squares * (1.0 / inner) + EPS)
        for tile in range(tiles):
            columns = slice(tile * TILE, (tile + 1) * TILE)
            gain = jnp.concatenate([gains[i : i + 1] for i in range(tile * per, (tile + 1) * per)], axis=1)
            nall[p, at, columns] = (ssd[at, columns] * scale * gain).astype(BF16)
        to_far(span).start()
        to_near(span).start()

    def settle(s, k):
        for from_left, there in ((True, me - s >= 0), (False, me + s < n)):

            @pl.when(there)
            def _():
                across(s, k, from_left, other).wait_recv()

    def gathered(span):
        to_near(span).wait_recv()
        far_to_near(span).wait_recv()

    def multiply(block, first=False):
        @pl.loop(0, o_ref.shape[1] // TILE)
        def _(tile):
            columns = pl.ds(pl.multiple_of(tile * TILE, TILE), TILE)
            part = dot(nall[block], wfull[pl.ds(pl.multiple_of(block * depth, 16), depth), columns])
            if first:
                total_ref[:, columns] = part
            else:
                total_ref[:, columns] += part

    def multiply_around(s):
        for k in range(chunks):
            settle(s, k)

        @pl.when(me - s >= 0)
        def _():
            multiply(me - s)

        @pl.when(me + s < n)
        def _():
            multiply(me + s)

    def relays(count):
        for _ in range(count):
            next_relay()

    stepwise = depth == inner
    relays(3)
    to_far(0).wait_recv()
    far_to_near(0).start()
    relays(3)
    to_far(1).wait_recv()
    far_to_near(1).start()
    own_copy.wait()
    relays(1)
    for span in range(spans):
        gathered(span)
    if stepwise:
        multiply(me, True)
        multiply_around(1)
        for s in range(2, n):
            while events and events[0][0] <= s:
                next_relay()
            multiply_around(s)
    else:
        while events:
            next_relay()

        @pl.loop(4, n)
        def _(s):
            for k in range(chunks):
                relay(s, k)

        @pl.loop(1, n)
        def _(s):
            for k in range(chunks):
                settle(s, k)

    def sent(s, k):
        for from_left, go, there in ((True, go_right, me - s >= 0), (False, go_left, me + s < n)):

            @pl.when(there)
            def _():
                across(s, k, from_left, g).wait_send()

                @pl.when(has_right if from_left else has_left)
                def _():
                    go(s, k).wait_send()

    @pl.when(has_right)
    def _():
        for tile in range(tiles):
            hand_on(tile).wait_send()
        for i in range(3):
            halo(i).wait_send()
        for k in range(chunks):
            go_right(0, k).wait_send()

    @pl.when(has_left)
    def _():
        for k in range(chunks):
            go_left(0, k).wait_send()

    for span in range(spans):
        to_near(span).wait_send()
        to_far(span).wait_send()
        far_to_near(span).wait_send()
    if n > 4:

        @pl.loop(1, n)
        def _(s):
            for k in range(chunks):
                sent(s, k)
    else:
        for s in range(1, n):
            for k in range(chunks):
                sent(s, k)

    @pl.loop(0, o_ref.shape[1] // TILE)
    def _(tile):
        columns = pl.ds(pl.multiple_of(tile * TILE, TILE), TILE)
        if stepwise:
            o_ref[:, columns] = total_ref[:, columns].astype(BF16)
        else:
            total = dot(nall[0], wfull[0:inner, columns])
            for block in range(1, 4):
                total = total + dot(nall[block], wfull[block * inner : (block + 1) * inner, columns])
            o_ref[:, columns] = total.astype(BF16)


def shards(
    x_in, z_in, b_in, c_in, dt_in, conv_x, conv_bc, dt_bias, a_log, d_skip, norm_gain, out_weight
):
    n = lax.axis_size("ctx")
    rows, inner = x_in.shape
    depth, out_columns = out_weight.shape
    assert lax.axis_size("tp") == 4 and lax.axis_size("groups") == 2
    assert b_in.shape[1] == STATE and rows == 2 * SPAN and conv_x.shape[0] == 4
    chunks = 4 if depth >= 256 else 1
    links = pltpu.SemaphoreType.DMA((n * chunks,))
    vmem = pl.BlockSpec(memory_space=pltpu.VMEM)
    operands = (
        x_in, z_in, b_in, c_in, dt_in.T, conv_x, conv_bc,
        dt_bias[None], a_log[None], d_skip[None], norm_gain.reshape(-1, 128),
    )
    return pl.pallas_call(
        functools.partial(kernel, n, chunks),
        out_shape=jax.ShapeDtypeStruct((rows, out_columns), BF16),
        in_specs=[pl.BlockSpec(memory_space=pltpu.HBM)] * 12,
        out_specs=vmem,
        scratch_shapes=[pltpu.VMEM(operand.shape, operand.dtype) for operand in operands]
        + [pltpu.SemaphoreType.DMA((len(operands),)), pltpu.VMEM((rows, out_columns), F32)]
        + [
            pltpu.VMEM((n * depth, out_columns), BF16),
            pltpu.VMEM((4, rows, inner), BF16),
            pltpu.VMEM((rows + 8, STATE), F32),
            pltpu.VMEM((rows, inner), BF16),
            pltpu.VMEM((rows, STATE), BF16),
            pltpu.VMEM((rows, STATE), BF16),
            pltpu.VMEM((rows, inner), F32),
            pltpu.VMEM((STATE, inner), F32),
            pltpu.VMEM((STATE, inner), F32),
            pltpu.VMEM((inner // TILE, STATE, TILE), BF16),
            pltpu.VMEM((inner // TILE, STATE, TILE), BF16),
            pltpu.VMEM((RIM, inner), BF16),
            pltpu.VMEM((RIM, STATE), BF16),
            pltpu.VMEM((RIM, STATE), BF16),
            pltpu.SemaphoreType.DMA,
            pltpu.SemaphoreType.DMA((3,)),
            pltpu.SemaphoreType.DMA((3,)),
            pltpu.SemaphoreType.DMA((inner // TILE,)),
            pltpu.SemaphoreType.DMA((inner // TILE,)),
        ]
        + [links] * 8
        + [pltpu.SemaphoreType.DMA((3, 2)), pltpu.SemaphoreType.DMA((3, 2))],
        compiler_params=pltpu.CompilerParams(
            collective_id=0, has_side_effects=True, vmem_limit_bytes=63 * 1024 * 1024
        ),
    )(*operands, out_weight)


def solution(mesh):
    rows = P(("groups", "ctx"), "tp")
    return jax.shard_map(
        shards,
        mesh=mesh,
        in_specs=(
            rows, rows, rows, rows, rows,
            P(None, "tp"), P(None, None, "tp"),
            P("tp"), P("tp"), P("tp"), P("tp"),
            P("ctx", "tp"),
        ),
        out_specs=rows,
        check_vma=False,
    )
```

```python
import functools
import jax
import jax.numpy as jnp
from jax import lax
from jax.experimental import pallas as pl
from jax.experimental.pallas import tpu as pltpu
from jax.sharding import PartitionSpec as P

STATE = 128
SPAN = 256
EPS = 1e-05
RIM = 16
TILE = 256
MESH = pl.DeviceIdType.MESH
F32 = jnp.float32
BF16 = jnp.bfloat16


def dot(a, b):
    return jnp.dot(a, b, preferred_element_type=F32)


def silu(v):
    return v / (1.0 + jnp.exp(-v))


def spread(value, table):
    high = value.astype(BF16)
    low = (value - high.astype(F32)).astype(BF16)
    return dot(high, table) + dot(low, table)


def kernel(
    n, chunks,
    x_hbm, z_hbm, b_hbm, c_hbm, dt_hbm, conv_hbm, convbc_hbm, bias_hbm, alog_hbm, skip_hbm, gain_hbm, w_ref,
    o_ref,
    x_ref, z_ref, b_ref, c_ref, dt_ref, conv_ref, convbc_ref, bias_ref, alog_ref, skip_ref, gain_ref, in_sem, total_ref,
    wfull, nall, xe, xs, bs, cs, ssd, state0, state1, entering, outgoing, halo_x, halo_b, halo_c,
    own_sem, halo_send, halo_recv, chain_send, chain_recv,
    right_send, right_recv, left_send, left_recv,
    yr_send, yr_recv, yl_send, yl_recv,
    tp_send, tp_recv,
):
    g = lax.axis_index("groups")
    me = lax.axis_index("ctx")
    p = lax.axis_index("tp")
    other = 1 - g
    near = p + 1 - 2 * lax.rem(p, 2)
    far = lax.rem(p + 2, 4)
    rows, inner = x_ref.shape
    heads = dt_ref.shape[0]
    width = inner // heads
    spans = rows // SPAN
    depth = w_ref.shape[0]
    half = depth // 2
    piece = half // chunks
    has_left, has_right = me > 0, me < n - 1

    sources = (x_hbm, z_hbm, b_hbm, c_hbm, dt_hbm, conv_hbm, convbc_hbm, bias_hbm, alog_hbm, skip_hbm, gain_hbm)
    held_in = (x_ref, z_ref, b_ref, c_ref, dt_ref, conv_ref, convbc_ref, bias_ref, alog_ref, skip_ref, gain_ref)
    loads = [
        pltpu.make_async_copy(source, to, in_sem.at[i]) for i, (source, to) in enumerate(zip(sources, held_in))
    ]
    barrier = pltpu.get_barrier_semaphore()
    for device in ({"groups": other}, {"tp": near}, {"tp": far}):
        pl.semaphore_signal(barrier, inc=1, device_id=device, device_id_type=MESH)

    @pl.when(has_left)
    def _():
        pl.semaphore_signal(barrier, inc=1, device_id={"ctx": me - 1}, device_id_type=MESH)

    @pl.when(has_right)
    def _():
        pl.semaphore_signal(barrier, inc=1, device_id={"ctx": me + 1}, device_id_type=MESH)

    for load in loads:
        load.start()
    pl.semaphore_wait(barrier, 3 + has_left.astype(jnp.int32) + has_right.astype(jnp.int32))

    def remote(src, dst, send, recv, device):
        return pltpu.make_async_remote_copy(
            src_ref=src, dst_ref=dst, send_sem=send, recv_sem=recv, device_id=device, device_id_type=MESH
        )

    def halo(i):
        src = (x_hbm, b_hbm, c_hbm)[i].at[pl.ds(rows - RIM, RIM)]
        dst = (halo_x, halo_b, halo_c)[i]
        return remote(src, dst, halo_send.at[i], halo_recv.at[i], {"ctx": me + 1})

    @pl.when(has_right)
    def _():
        for i in range(3):
            halo(i).start()

    def strip(block, part, k):
        return pl.ds(pl.multiple_of(block * depth + part * half + k * piece, 16), piece)

    def own_strip(k):
        return pl.ds(pl.multiple_of(g * half + k * piece, 16), piece)

    def go_right(s, k):
        src = w_ref.at[own_strip(k)] if isinstance(s, int) and s == 0 else wfull.at[strip(me - s, g, k)]
        return remote(
            src, wfull.at[strip(me - s, g, k)],
            right_send.at[s * chunks + k], right_recv.at[s * chunks + k], {"ctx": me + 1},
        )

    def go_left(s, k):
        src = w_ref.at[own_strip(k)] if isinstance(s, int) and s == 0 else wfull.at[strip(me + s, g, k)]
        return remote(
            src, wfull.at[strip(me + s, g, k)],
            left_send.at[s * chunks + k], left_recv.at[s * chunks + k], {"ctx": me - 1},
        )

    def arrival(s, k, from_left):
        at = strip(me - s if from_left else me + s, g, k)
        send, recv = (right_send, right_recv) if from_left else (left_send, left_recv)
        spot = (s - 1) * chunks + k
        return remote(
            wfull.at[at], wfull.at[at], send.at[spot], recv.at[spot], {"ctx": me}
        )

    def across(s, k, from_left, part):
        at = strip(me - s if from_left else me + s, part, k)
        send, recv = (yr_send, yr_recv) if from_left else (yl_send, yl_recv)
        spot = (s - 1) * chunks + k
        return remote(wfull.at[at], wfull.at[at], send.at[spot], recv.at[spot], {"groups": other})

    early = chunks // 2 + me * (chunks // 4) if chunks > 1 else 1
    for k in range(chunks):

        @pl.when(jnp.logical_and(has_right, k < early))
        def _():
            go_right(0, k).start()

        @pl.when(has_left)
        def _():
            go_left(0, k).start()

    own_copy = pltpu.make_async_copy(
        w_ref, wfull.at[pl.ds(pl.multiple_of(me * depth, 16), depth)], own_sem
    )
    own_copy.start()

    def onward(s, k):
        @pl.when(jnp.logical_and(me - s >= 0, has_right))
        def _():
            go_right(s, k).start()

    def relay(s, k, hold=False):
        @pl.when(me + s < n)
        def _():
            arrival(s, k, False).wait_recv()

            @pl.when(has_left)
            def _():
                go_left(s, k).start()

            across(s, k, False, g).start()

        @pl.when(me - s >= 0)
        def _():
            arrival(s, k, True).wait_recv()
            across(s, k, True, g).start()

        if not hold:
            onward(s, k)

    events = [(s, k) for s in range(1, min(n, 4)) for k in range(chunks)]

    held_back = []

    def next_relay(hold=False):
        if events:
            if hold:
                held_back.append(events[0])
            relay(*events.pop(0), hold)

    for i in (2, 3, 0, 4, 5, 6, 7, 8):
        loads[i].wait()

    @pl.when(jnp.logical_not(has_left))
    def _():
        halo_x[...] = jnp.zeros_like(halo_x)
        halo_b[...] = jnp.zeros_like(halo_b)
        halo_c[...] = jnp.zeros_like(halo_c)

    @pl.when(has_left)
    def _():
        for i in range(3):
            halo(i).wait_recv()

    def conv(src, rim, taps, dst, columns):
        xe[0:8] = rim[:, columns].astype(F32)[RIM - 8 :]
        xe[8 : 8 + rows] = src[:, columns].astype(F32)
        weights = taps(columns).astype(F32)
        for first in range(0, rows, 128):
            total = xe[first + 5 : first + 5 + 128] * weights[0:1]
            for tap in range(1, 4):
                total = total + xe[first + 5 + tap : first + 5 + tap + 128] * weights[tap : tap + 1]
            dst[first : first + 128, columns] = silu(total).astype(BF16)

    every = pl.ds(0, STATE)
    conv(b_ref, halo_b, lambda cols: convbc_ref[0, :, cols], bs, every)
    conv(c_ref, halo_c, lambda cols: convbc_ref[1, :, cols], cs, every)

    @pl.loop(0, inner // STATE)
    def _(tile):
        columns = pl.ds(pl.multiple_of(tile * STATE, STATE), STATE)
        conv(x_ref, halo_x, lambda cols: conv_ref[:, cols], xs, columns)

    raw = dt_ref[...].astype(F32).T + bias_ref[...]
    step = jnp.maximum(raw, 0.0) + jnp.log1p(jnp.exp(-jnp.abs(raw)))
    log_decay = -jnp.exp(alog_ref[...]) * step
    t_at = lax.broadcasted_iota(jnp.int32, (SPAN, SPAN), 0)
    s_at = lax.broadcasted_iota(jnp.int32, (SPAN, SPAN), 1)
    causal = t_at >= s_at
    lower = causal.astype(F32)
    eye = (
        lax.broadcasted_iota(jnp.int32, (heads, heads), 0) == lax.broadcasted_iota(jnp.int32, (heads, heads), 1)
    ).astype(F32)

    def turned(value):
        return lax.dot_general(
            eye, value, (((1,), (1,)), ((), ())), precision=lax.Precision.HIGHEST, preferred_element_type=F32
        )

    def table(tile):
        channel = lax.broadcasted_iota(jnp.int32, (heads, TILE), 1) + tile * TILE
        first = lax.broadcasted_iota(jnp.int32, (heads, TILE), 0) * width
        return jnp.logical_and(channel >= first, channel < first + width).astype(BF16)

    tiles = inner // TILE
    tables = [table(tile) for tile in range(tiles)]
    states = (state0, state1)
    steps, cums, ends = [], [], []
    for span in range(spans):
        at = slice(span * SPAN, (span + 1) * SPAN)
        step_here = step[at]
        cum = jnp.dot(lower, log_decay[at], precision=lax.Precision.HIGHEST, preferred_element_type=F32)
        steps.append(step_here)
        cums.append(cum)
        to_end = jnp.exp(cum[SPAN - 1 : SPAN] - cum) * step_here
        b_turned = bs[at].astype(F32).T.astype(BF16)
        decay = []
        for tile in range(tiles):
            columns = slice(tile * TILE, (tile + 1) * TILE)
            weighted = (xs[at, columns].astype(F32) * spread(to_end, tables[tile])).astype(BF16)
            states[span][:, columns] = dot(b_turned, weighted)
            decay.append(spread(jnp.exp(cum[SPAN - 8 :]), tables[tile])[7:8])
        ends.append(decay)

    def hand_on(tile):
        return remote(
            outgoing.at[tile], entering.at[tile], chain_send.at[tile], chain_recv.at[tile], {"ctx": me + 1}
        )

    def pass_on(tile, first):
        columns = slice(tile * TILE, (tile + 1) * TILE)
        total = ends[1][tile] * state0[:, columns] + state1[:, columns]
        if not first:
            total = total + ends[0][tile] * ends[1][tile] * entering[tile].astype(F32)
        outgoing[tile] = total.astype(BF16)
        hand_on(tile).start()

    @pl.when(jnp.logical_not(has_left))
    def _():
        entering[...] = jnp.zeros_like(entering)
        for tile in range(tiles):
            pass_on(tile, True)

    def chain_relay(tile):
        @pl.when(has_left)
        def _():
            hand_on(tile).wait_recv()

            @pl.when(has_right)
            def _():
                pass_on(tile, False)

    low_lane = lax.broadcasted_iota(jnp.int32, (128, 2 * width), 1) < width
    done = 0
    for span in range(spans):
        base = span * SPAN
        scores = lax.dot_general(
            cs[base : base + SPAN], bs[base : base + SPAN], (((1,), (1,)), ((), ())), preferred_element_type=F32
        )
        scores = jnp.where(causal, scores, 0.0)
        cum = cums[span]
        cum_turned = turned(cum)
        step_turned = turned(steps[span])
        for pair in range(heads // 2):
            columns = slice(pair * 2 * width, (pair + 1) * 2 * width)
            for block in range(2):
                top, reach = block * 128, (block + 1) * 128
                parts = []
                for head in (2 * pair, 2 * pair + 1):
                    gap = cum[top:reach, head : head + 1] - cum_turned[head : head + 1, :reach]
                    mixing = (
                        scores[top:reach, :reach] * jnp.exp(jnp.minimum(gap, 0.0))
                        * step_turned[head : head + 1, :reach]
                    ).astype(BF16)
                    parts.append(dot(mixing, xs[base : base + reach, columns]))
                ssd[base + top : base + reach, columns] = jnp.where(low_lane, parts[0], parts[1])
            done += 1
            if done in (6, 9, 12) and chunks > 1:
                next_relay(True)

    for tile in range(tiles):
        chain_relay(tile)
    for k in range(chunks):

        @pl.when(jnp.logical_and(has_right, k >= early))
        def _():
            go_right(0, k).start()

    for s, k in held_back:
        onward(s, k)
    for _ in range(3):
        next_relay()

    loads[1].wait()
    loads[9].wait()
    loads[10].wait()

    blocks = lambda block, span: nall.at[block, pl.ds(span * SPAN, SPAN)]

    def to_near(span):
        return remote(blocks(p, span), blocks(p, span), tp_send.at[0, span], tp_recv.at[0, span], {"tp": near})

    def to_far(span):
        return remote(blocks(p, span), blocks(p, span), tp_send.at[1, span], tp_recv.at[1, span], {"tp": far})

    def far_to_near(span):
        return remote(blocks(far, span), blocks(far, span), tp_send.at[2, span], tp_recv.at[2, span], {"tp": near})

    gains, per = gain_ref[...].astype(F32), TILE // 128
    skips = [spread(skip_ref[...] + jnp.zeros((8, heads), F32), tables[tile])[0:1] for tile in range(tiles)]
    for span in range(spans):
        at = slice(span * SPAN, (span + 1) * SPAN)
        growth = jnp.exp(cums[span])
        squares = jnp.zeros((SPAN, 1), F32)
        for tile in range(tiles):
            columns = slice(tile * TILE, (tile + 1) * TILE)
            held = entering[tile].astype(F32)
            if span == 0:
                carried = dot(cs[at], entering[tile])
            else:
                held = ends[0][tile] * held + state0[:, columns]
                high = held.astype(BF16)
                carried = dot(cs[at], high) + dot(cs[at], (held - high.astype(F32)).astype(BF16))
            full = ssd[at, columns] + carried * spread(growth, tables[tile])
            full = full + skips[tile] * xs[at, columns].astype(F32)
            gated = full * silu(z_ref[at, columns].astype(F32))
            ssd[at, columns] = gated
            squares = squares + jnp.sum(gated * gated, axis=1, keepdims=True)
        scale = lax.rsqrt(squares * (1.0 / inner) + EPS)
        for tile in range(tiles):
            columns = slice(tile * TILE, (tile + 1) * TILE)
            gain = jnp.concatenate([gains[i : i + 1] for i in range(tile * per, (tile + 1) * per)], axis=1)
            nall[p, at, columns] = (ssd[at, columns] * scale * gain).astype(BF16)
        to_far(span).start()
        to_near(span).start()

    def settle(s, k):
        for from_left, there in ((True, me - s >= 0), (False, me + s < n)):

            @pl.when(there)
            def _():
                across(s, k, from_left, other).wait_recv()

    def gathered(span):
        to_near(span).wait_recv()
        far_to_near(span).wait_recv()

    def multiply(block, first=False):
        @pl.loop(0, o_ref.shape[1] // TILE)
        def _(tile):
            columns = pl.ds(pl.multiple_of(tile * TILE, TILE), TILE)
            part = dot(nall[block], wfull[pl.ds(pl.multiple_of(block * depth, 16), depth), columns])
            if first:
                total_ref[:, columns] = part
            else:
                total_ref[:, columns] += part

    def multiply_around(s):
        for k in range(chunks):
            settle(s, k)

        @pl.when(me - s >= 0)
        def _():
            multiply(me - s)

        @pl.when(me + s < n)
        def _():
            multiply(me + s)

    def relays(count):
        for _ in range(count):
            next_relay()

    stepwise = depth == inner
    relays(5)
    to_far(0).wait_recv()
    far_to_near(0).start()
    relays(5)
    to_far(1).wait_recv()
    far_to_near(1).start()
    own_copy.wait()
    relays(3)
    for span in range(spans):
        gathered(span)
    if stepwise:
        multiply(me, True)
        multiply_around(1)
        for s in range(2, n):
            while events and events[0][0] <= s:
                next_relay()
            multiply_around(s)
    else:
        while events:
            next_relay()

        @pl.loop(4, n)
        def _(s):
            for k in range(chunks):
                relay(s, k)

        @pl.loop(1, n)
        def _(s):
            for k in range(chunks):
                settle(s, k)

    def sent(s, k):
        for from_left, go, there in ((True, go_right, me - s >= 0), (False, go_left, me + s < n)):

            @pl.when(there)
            def _():
                across(s, k, from_left, g).wait_send()

                @pl.when(has_right if from_left else has_left)
                def _():
                    go(s, k).wait_send()

    @pl.when(has_right)
    def _():
        for tile in range(tiles):
            hand_on(tile).wait_send()
        for i in range(3):
            halo(i).wait_send()
        for k in range(chunks):
            go_right(0, k).wait_send()

    @pl.when(has_left)
    def _():
        for k in range(chunks):
            go_left(0, k).wait_send()

    for span in range(spans):
        to_near(span).wait_send()
        to_far(span).wait_send()
        far_to_near(span).wait_send()
    if n > 4:

        @pl.loop(1, n)
        def _(s):
            for k in range(chunks):
                sent(s, k)
    else:
        for s in range(1, n):
            for k in range(chunks):
                sent(s, k)

    @pl.loop(0, o_ref.shape[1] // TILE)
    def _(tile):
        columns = pl.ds(pl.multiple_of(tile * TILE, TILE), TILE)
        if stepwise:
            o_ref[:, columns] = total_ref[:, columns].astype(BF16)
        else:
            total = dot(nall[0], wfull[0:inner, columns])
            for block in range(1, 4):
                total = total + dot(nall[block], wfull[block * inner : (block + 1) * inner, columns])
            o_ref[:, columns] = total.astype(BF16)


def shards(
    x_in, z_in, b_in, c_in, dt_in, conv_x, conv_bc, dt_bias, a_log, d_skip, norm_gain, out_weight
):
    n = lax.axis_size("ctx")
    rows, inner = x_in.shape
    depth, out_columns = out_weight.shape
    assert lax.axis_size("tp") == 4 and lax.axis_size("groups") == 2
    assert b_in.shape[1] == STATE and rows == 2 * SPAN and conv_x.shape[0] == 4
    chunks = 8 if depth >= 256 else 1
    links = pltpu.SemaphoreType.DMA((n * chunks,))
    vmem = pl.BlockSpec(memory_space=pltpu.VMEM)
    operands = (
        x_in, z_in, b_in, c_in, dt_in.T, conv_x, conv_bc,
        dt_bias[None], a_log[None], d_skip[None], norm_gain.reshape(-1, 128),
    )
    return pl.pallas_call(
        functools.partial(kernel, n, chunks),
        out_shape=jax.ShapeDtypeStruct((rows, out_columns), BF16),
        in_specs=[pl.BlockSpec(memory_space=pltpu.HBM)] * 12,
        out_specs=vmem,
        scratch_shapes=[pltpu.VMEM(operand.shape, operand.dtype) for operand in operands]
        + [pltpu.SemaphoreType.DMA((len(operands),)), pltpu.VMEM((rows, out_columns), F32)]
        + [
            pltpu.VMEM((n * depth, out_columns), BF16),
            pltpu.VMEM((4, rows, inner), BF16),
            pltpu.VMEM((rows + 8, STATE), F32),
            pltpu.VMEM((rows, inner), BF16),
            pltpu.VMEM((rows, STATE), BF16),
            pltpu.VMEM((rows, STATE), BF16),
            pltpu.VMEM((rows, inner), F32),
            pltpu.VMEM((STATE, inner), F32),
            pltpu.VMEM((STATE, inner), F32),
            pltpu.VMEM((inner // TILE, STATE, TILE), BF16),
            pltpu.VMEM((inner // TILE, STATE, TILE), BF16),
            pltpu.VMEM((RIM, inner), BF16),
            pltpu.VMEM((RIM, STATE), BF16),
            pltpu.VMEM((RIM, STATE), BF16),
            pltpu.SemaphoreType.DMA,
            pltpu.SemaphoreType.DMA((3,)),
            pltpu.SemaphoreType.DMA((3,)),
            pltpu.SemaphoreType.DMA((inner // TILE,)),
            pltpu.SemaphoreType.DMA((inner // TILE,)),
        ]
        + [links] * 8
        + [pltpu.SemaphoreType.DMA((3, 2)), pltpu.SemaphoreType.DMA((3, 2))],
        compiler_params=pltpu.CompilerParams(
            collective_id=0, has_side_effects=True, vmem_limit_bytes=63 * 1024 * 1024
        ),
    )(*operands, out_weight)


def solution(mesh):
    rows = P(("groups", "ctx"), "tp")
    return jax.shard_map(
        shards,
        mesh=mesh,
        in_specs=(
            rows, rows, rows, rows, rows,
            P(None, "tp"), P(None, None, "tp"),
            P("tp"), P("tp"), P("tp"), P("tp"),
            P("ctx", "tp"),
        ),
        out_specs=rows,
        check_vma=False,
    )
```
